32 devices in a mesh: grp: 2 (over x), fin: 8 (over z, y), fout: 2 (over core).
Axes of the slice: x: 2, y: 2, z: 4, core: 2. Of those that a mesh axis runs over, the one named last changes fastest.
Arguments:
- tokens: bfloat16 [512, 6144], P(('grp', 'fin'), 'fout'), parts along dimension 0, may hold values from -6 to 6
- w_up: bfloat16 [6144, 24576], P('fout', 'fin'), may hold values from -0.078125 to 0.078125
- w_down: bfloat16 [24576, 6144], P('fin', 'fout'), may hold values from -0.0390625 to 0.0390625
- up_scale: float32 [8, 24576], P(None, 'fin'), may hold values from 0.25 to 4
- down_scale: float32 [8, 6144], P(None, 'fout'), may hold values from 0.25 to 4
- step_group: int32 [16], P('grp'), parts along dimension 0, may hold values from 0 to 7
- req_lengths: int32 [16], P('grp'), parts along dimension 0, may hold values from 1 to 64, 256 in all
Outputs:
- mixed: bfloat16 [512, 6144], P(('grp', 'fin'), 'fout'), parts along dimension 0
The draws below stay inside these ranges and needn't reach their ends.
There are 2 independent parts, one for each index of `grp`. The reference program is written for one: setup_inputs(seed, part) draws one part's arguments, and reference() takes and returns one part's arrays. A program takes and returns all parts, laid end to end along the dimension named above; an argument that names none is the same for every part. Nothing has to cross between parts.
Inputs may be any that keep to these rules, and one draw needn't show every extreme that they name: `req_lengths`: the lengths sum to 256.
All inputs are finite; a program needn't handle non-finite values.
Results may differ from the reference program's by a relative error of at most 0.005.
Values may be sent and summed in bfloat16 or wider, within the bound.
No kernel may reach another device: no remote copies, remote signals or barrier semaphores. Data moves between devices by JAX's collectives and lax.ppermute only.
A program may use at most 128 MiB of HBM per device.

```python
import math
import jax
import jax.numpy as jnp
import numpy as np
from jax import lax

D = 6144
FF = 24576
GROUPS = 8
REQS = 8
TOKENS = 256


def set_ends(values, own_key, low, top_value):
    longest = values.shape.index(max(values.shape))
    spots = []
    for shift in (0, 1):
        where = [jax.random.randint(jax.random.fold_in(own_key, axis), (), 0, length) for axis, length in enumerate(values.shape)]
        where[longest] = (where[longest] + shift) % values.shape[longest]
        spots.append(tuple(where))
    return values.at[spots[0]].set(low).at[spots[1]].set(top_value)


def block_scale(own_key, dims, shards, low, high):
    def one(position, shards_of):
        steps = jax.random.uniform(jax.random.fold_in(jax.random.fold_in(own_key, 6), position), (shards_of,), jnp.float32, low / len(shards), high / len(shards))
        return jnp.repeat(jnp.exp(steps), dims[position] // shards_of).reshape((-1,) + (1,) * (len(dims) - position - 1))

    loudness = one(*shards[0])
    for cut in shards[1:]:
        loudness = loudness * one(*cut)
    return loudness


def split_up(number_of, total, bound, slope):
    loads = [(1 << 20) // math.isqrt(rank ** slope) + 1 for rank in range(2, number_of + 1)]
    surplus, given = total - bound - (number_of - 1), [1] * (number_of - 1)
    while surplus > 0:
        free = [i for i in range(number_of - 1) if given[i] < bound]
        pool, budget = sum([loads[i] for i in free]), surplus
        for i in free:
            extra = min(bound - given[i], max(1, budget * loads[i] // pool), surplus)
            given[i] = given[i] + extra
            surplus = surplus - extra
    return np.array([bound] + given)


def uneven(own_key, count, total, most, slope):
    if count == 2:
        one = jax.random.randint(own_key, (), max(1, total - most), min(most, total - 1) + 1)
        return jnp.stack([one, total - one])
    sizes = jnp.asarray(split_up(count, total, most, slope), jnp.int32)
    pairs = (count - 1) // 2
    donor, receiver = sizes[1:1 + 2 * pairs:2], sizes[2:2 + 2 * pairs:2]
    room = jnp.minimum(donor - 1, most - receiver)
    moved = jax.random.randint(jax.random.fold_in(own_key, 1), (pairs,), 0, 1 << 20) % (room + 1)
    sizes = sizes.at[1:1 + 2 * pairs:2].set(donor - moved).at[2:2 + 2 * pairs:2].set(receiver + moved)
    return sizes[jax.random.permutation(jax.random.fold_in(own_key, 2), count)]


def gaussian(own_key, dims, width, bound, pieces=(), kind=jnp.bfloat16):
    array = jax.random.normal(own_key, dims, jnp.float32) * width
    if len(pieces) > 0:
        array = block_scale(own_key, dims, pieces, -0.22, 0.18) * array
    return jnp.clip(array, min=-bound, max=bound).astype(kind)


def setup_inputs(seed: int = 0, part: int = 0) -> dict:
    key_of = jax.random.split(jax.random.key(seed), 8)
    part_keys = jax.random.split(jax.random.fold_in(key_of[7], part), 8)
    tokens = gaussian(part_keys[0], (TOKENS, D), 1.0, 6.0, ((0, 8), (1, 2)))
    w_up = gaussian(key_of[1], (D, FF), D ** -0.5, 0.078125, ((0, 2), (1, 8)))
    w_down = gaussian(key_of[2], (FF, D), FF ** -0.5, 0.0390625, ((0, 8), (1, 2)))
    up_scale = jnp.clip(jnp.exp(math.log(4.0) - 2.7725887 * jax.random.uniform(key_of[3], (GROUPS, FF), jnp.float32) ** block_scale(key_of[3], (GROUPS, FF), ((1, 8),), -0.2, 0.2)), 0.25, 4.0)
    down_scale = jnp.clip(jnp.exp(math.log(4.0) - 2.7725887 * jax.random.uniform(key_of[4], (GROUPS, D), jnp.float32) ** block_scale(key_of[4], (GROUPS, D), ((1, 2),), -0.2, 0.2)), 0.25, 4.0)
    step_group = set_ends(jax.random.randint(part_keys[5], (REQS,), 0, GROUPS), jax.random.fold_in(part_keys[5], 1), 0, GROUPS - 1).astype(jnp.int32)
    req_lengths = uneven(part_keys[6], REQS, TOKENS, TOKENS // 4, 2).astype(jnp.int32)
    return dict(tokens=tokens, w_up=w_up, w_down=w_down, up_scale=up_scale, down_scale=down_scale, step_group=step_group, req_lengths=req_lengths)


def group_table(count, req_lengths, step_group):
    rows = jnp.arange(count, dtype=jnp.int32)
    ends = jnp.cumsum(req_lengths).astype(jnp.int32)
    request = jnp.sum((rows[:, None] >= ends[None, :]).astype(jnp.int32), axis=1)
    picked = (request[:, None] == jnp.arange(REQS, dtype=jnp.int32)[None, :]).astype(jnp.int32)
    row_group = jnp.sum(picked * step_group[None, :], axis=1).astype(jnp.int32)
    return (row_group[:, None] == jnp.arange(GROUPS, dtype=jnp.int32)[None, :]).astype(jnp.float32)


def reference(tokens, w_up, w_down, up_scale, down_scale, step_group, req_lengths):
    onehot = group_table(TOKENS, req_lengths, step_group)
    pre = jnp.dot(tokens, w_up, preferred_element_type=jnp.float32)
    scale_one = jnp.dot(onehot, up_scale, precision=lax.Precision.HIGHEST)
    hidden = jax.nn.gelu(pre * scale_one, approximate=True).astype(jnp.bfloat16)
    terms = jnp.dot(hidden, w_down, preferred_element_type=jnp.float32)
    scale_two = jnp.dot(onehot, down_scale, precision=lax.Precision.HIGHEST)
    return (terms * scale_two).astype(jnp.bfloat16)
```

```python
import jax
import jax.numpy as jnp
from jax import lax
from jax.sharding import PartitionSpec as P


def group_table(rows, req_lengths, step_group, groups):
    ends = jnp.cumsum(req_lengths)
    request = jnp.sum((rows[:, None] >= ends[None, :]).astype(jnp.int32), axis=1)
    picked = (
        request[:, None] == jnp.arange(req_lengths.shape[0], dtype=jnp.int32)[None, :]
    ).astype(jnp.int32)
    row_group = jnp.sum(picked * step_group[None, :], axis=1)
    return (row_group[:, None] == jnp.arange(groups, dtype=jnp.int32)[None, :]).astype(jnp.float32)


def scales(rows, req_lengths, step_group, table):
    onehot = group_table(rows, req_lengths, step_group, table.shape[0]).astype(jnp.bfloat16)
    high = table.astype(jnp.bfloat16)
    rest = table - high.astype(jnp.float32)
    middle = rest.astype(jnp.bfloat16)
    low = (rest - middle.astype(jnp.float32)).astype(jnp.bfloat16)
    return jnp.dot(
        jnp.concatenate([onehot] * 3, axis=1),
        jnp.concatenate([high, middle, low], axis=0),
        preferred_element_type=jnp.float32,
    )


def by_collectives(tokens, w_up, w_down, up_scale, down_scale, step_group, req_lengths):
    pre = jnp.dot(
        lax.all_gather(tokens, "fin", axis=0, tiled=True), w_up, preferred_element_type=jnp.float32
    )
    total_rows = pre.shape[0]
    half_sum = lax.psum_scatter(pre, "fout", scatter_dimension=0, tiled=True)
    half_rows = half_sum.shape[0]
    rows = lax.axis_index("fout") * half_rows + jnp.arange(half_rows, dtype=jnp.int32)
    scale_one = scales(rows, req_lengths, step_group, up_scale)
    half_hidden = jax.nn.gelu(half_sum * scale_one, approximate=True).astype(jnp.bfloat16)
    hidden = lax.all_gather(half_hidden, "fout", axis=0, tiled=True)
    summed_rows = lax.psum_scatter(
        jnp.dot(hidden, w_down, preferred_element_type=jnp.float32),
        "fin",
        scatter_dimension=0,
        tiled=True,
    )
    own_rows = total_rows // lax.axis_size("fin")
    rows = lax.axis_index("fin") * own_rows + jnp.arange(own_rows, dtype=jnp.int32)
    scale_two = scales(rows, req_lengths, step_group, down_scale)
    return (summed_rows * scale_two).astype(jnp.bfloat16)


ACROSS = [(z * 2 + y, z * 2 + 1 - y) for z in range(4) for y in range(2)]


def move_y(x):
    return lax.ppermute(x, "fin", ACROSS)


def fetch_z(x, k):
    return lax.ppermute(
        x, "fin", [((z + k) % 4 * 2 + y, z * 2 + y) for z in range(4) for y in range(2)]
    )


def send_z(x, k):
    return lax.ppermute(
        x, "fin", [(z * 2 + y, (z + k) % 4 * 2 + y) for z in range(4) for y in range(2)]
    )


def gather(tokens, width):
    own = tokens
    across = move_y(own)
    singles = [fetch_z(own[:, :width], k) for k in (1, 2, 3)]
    pair = jnp.stack([own[:, width:], across[:, width:]])
    pairs = [fetch_z(pair, k) for k in (1, 2, 3)]
    single_pairs = [move_y(x) for x in singles]
    left = jnp.concatenate([own[:, :width], *singles, across[:, :width], *single_pairs])
    right = jnp.concatenate(
        [own[:, width:], *[p[0] for p in pairs], across[:, width:], *[p[1] for p in pairs]]
    )
    return left, right


def wide(x):
    return x.astype(jnp.float32)


def scatter(over_y, over_z):
    half = jnp.bfloat16
    rows = over_y.shape[0] // 8
    b = over_y.reshape(2, 4, rows, -1)
    a = over_z.reshape(2, 4, rows, -1)
    a_moved = [send_z(a[:, k].astype(half), k) for k in (1, 2, 3)]
    b_across = move_y(b[1, 1:].astype(half))
    b_moved = [
        send_z((b[0, k] + wide(b_across[k - 1])).astype(half), k) for k in (1, 2, 3)
    ]
    a_sum = a[:, 0] + wide(a_moved[0]) + wide(a_moved[1]) + wide(a_moved[2])
    last = move_y(jnp.concatenate([b[1, 0], a_sum[1]], axis=1).astype(half))
    b_sum = b[0, 0] + wide(b_moved[0]) + wide(b_moved[1]) + wide(b_moved[2])
    return jnp.concatenate([b_sum, a_sum[0]], axis=1) + wide(last)


def by_permutes(tokens, w_up, w_down, up_scale, down_scale, step_group, req_lengths):
    place = lax.axis_index("fin")
    z, y = place // 2, place % 2
    own_rows, depth = tokens.shape

    k, j = jnp.arange(4, dtype=jnp.int32), jnp.arange(2, dtype=jnp.int32)
    block = ((z + k) % 4)[None, :] * 2 + (y ^ j)[:, None]
    rows = block.reshape(-1, 1) * own_rows + jnp.arange(own_rows, dtype=jnp.int32)[None, :]
    scale_one = scales(rows.reshape(-1), req_lengths, step_group, up_scale)
    scale_two = scales(rows[0], req_lengths, step_group, down_scale)

    width = depth * 3 // 4 // 128 * 128
    left, right = gather(tokens, width)
    pre = jnp.dot(left, w_up[:width], preferred_element_type=jnp.float32)
    pre = pre + jnp.dot(right, w_up[width:], preferred_element_type=jnp.float32)
    other = lax.ppermute(pre.astype(jnp.bfloat16), "fout", [(0, 1), (1, 0)])
    hidden = jax.nn.gelu((pre + wide(other)) * scale_one, approximate=True)
    hidden = hidden.astype(jnp.bfloat16)
    width = w_down.shape[1] * 3 // 4 // 128 * 128
    over_z = jnp.dot(hidden, w_down[:, width:], preferred_element_type=jnp.float32)
    over_y = jnp.dot(hidden, w_down[:, :width], preferred_element_type=jnp.float32)
    return (scatter(over_y, over_z) * scale_two).astype(jnp.bfloat16)


def solution(mesh):
    on_device = by_permutes if mesh.shape["fin"] == 8 else by_collectives
    return jax.shard_map(
        on_device,
        mesh=mesh,
        in_specs=(
            P(("grp", "fin"), "fout"),
            P("fout", "fin"),
            P("fin", "fout"),
            P(None, "fin"),
            P(None, "fout"),
            P("grp"),
            P("grp"),
        ),
        out_specs=P(("grp", "fin"), "fout"),
        check_vma=False,
    )
```

```python
import math
import jax
import jax.numpy as jnp
from jax import lax
from jax.experimental import pallas as pl
from jax.experimental.pallas import tpu as pltpu
from jax.sharding import PartitionSpec as P


def group_table(rows, req_lengths, step_group, groups):
    place = jnp.arange(req_lengths.shape[0], dtype=jnp.int32)
    before = place[None, :] < place[:, None]
    starts = jnp.sum(jnp.where(before, req_lengths[None, :], 0), axis=1)
    ends = starts + req_lengths
    held = (rows[:, None] >= starts[None, :]) & (rows[:, None] < ends[None, :])
    row_group = jnp.sum(jnp.where(held, step_group[None, :], 0), axis=1)
    return (row_group[:, None] == jnp.arange(groups, dtype=jnp.int32)[None, :]).astype(jnp.float32)


def scales(rows, req_lengths, step_group, table):
    onehot = group_table(rows, req_lengths, step_group, table.shape[0]).astype(jnp.bfloat16)
    high = lax.reduce_precision(table, 8, 7)
    middle = lax.reduce_precision(table - high, 8, 7)
    low = table - high - middle
    return jnp.dot(
        jnp.concatenate([onehot] * 3, axis=1),
        jnp.concatenate([high, middle, low], axis=0).astype(jnp.bfloat16),
        preferred_element_type=jnp.float32,
    )


def by_collectives(tokens, w_up, w_down, up_scale, down_scale, step_group, req_lengths):
    pre = jnp.dot(
        lax.all_gather(tokens, "fin", axis=0, tiled=True), w_up, preferred_element_type=jnp.float32
    )
    total_rows = pre.shape[0]
    half_sum = lax.psum_scatter(pre, "fout", scatter_dimension=0, tiled=True)
    half_rows = half_sum.shape[0]
    rows = lax.axis_index("fout") * half_rows + jnp.arange(half_rows, dtype=jnp.int32)
    scale_one = scales(rows, req_lengths, step_group, up_scale)
    half_hidden = jax.nn.gelu(half_sum * scale_one, approximate=True).astype(jnp.bfloat16)
    hidden = lax.all_gather(half_hidden, "fout", axis=0, tiled=True)
    summed_rows = lax.psum_scatter(
        jnp.dot(hidden, w_down, preferred_element_type=jnp.float32),
        "fin",
        scatter_dimension=0,
        tiled=True,
    )
    own_rows = total_rows // lax.axis_size("fin")
    rows = lax.axis_index("fin") * own_rows + jnp.arange(own_rows, dtype=jnp.int32)
    scale_two = scales(rows, req_lengths, step_group, down_scale)
    return (summed_rows * scale_two).astype(jnp.bfloat16)


ACROSS = [(z * 2 + y, z * 2 + 1 - y) for z in range(4) for y in range(2)]


def move_y(x):
    return lax.ppermute(x, "fin", ACROSS)


def fetch_z(x, k):
    return lax.ppermute(
        x, "fin", [((z + k) % 4 * 2 + y, z * 2 + y) for z in range(4) for y in range(2)]
    )


def send_z(x, k):
    return lax.ppermute(
        x, "fin", [(z * 2 + y, (z + k) % 4 * 2 + y) for z in range(4) for y in range(2)]
    )


def wide(x):
    return x.astype(jnp.float32)


VMEM = pl.BlockSpec(memory_space=pltpu.VMEM)
HBM = pl.BlockSpec(memory_space=pltpu.HBM)
ANY = pl.BlockSpec(memory_space=pl.ANY)
TILE = 512
AHEAD = 3


def params(mib):
    return pltpu.CompilerParams(vmem_limit_bytes=mib * 2**20)


def dot(a, b):
    return jnp.dot(a, b, preferred_element_type=jnp.float32)


def load_kernel(*refs):
    w_ref, out_ref, sems = refs[0], refs[-2], refs[-1]
    step = out_ref.shape[0] // sems.shape[0]
    moving = [
        pltpu.make_async_copy(
            w_ref.at[pl.ds(i * step, step)], out_ref.at[pl.ds(i * step, step)], sems.at[i]
        )
        for i in range(sems.shape[0])
    ]
    for c in moving:
        c.start()
    for c in moving:
        c.wait()


def load(w, after):
    return pl.pallas_call(
        load_kernel,
        in_specs=[HBM] + [ANY] * len(after),
        out_specs=VMEM,
        out_shape=pltpu.VMEM(w.shape, w.dtype),
        scratch_shapes=[pltpu.SemaphoreType.DMA((4,))],
        compiler_params=params(2),
        cost_estimate=pl.CostEstimate(flops=0, bytes_accessed=4 * w.size, transcendentals=0),
    )(w, *after)


def up_kernel(start, x_ref, w_ref, out_ref):
    for lo in range(0, out_ref.shape[1], TILE):
        at = slice(start + lo, start + lo + TILE)
        out_ref[:, lo : lo + TILE] = dot(x_ref[...], w_ref[:, at])


def up(x, w, start, count):
    rows = x.shape[0]
    return pl.pallas_call(
        lambda *refs: up_kernel(start, *refs),
        in_specs=[VMEM] * 2,
        out_specs=VMEM,
        out_shape=jax.ShapeDtypeStruct((rows, count), jnp.float32),
        compiler_params=params(2),
        cost_estimate=pl.CostEstimate(
            flops=2 * rows * w.shape[0] * count, bytes_accessed=4 * rows * count, transcendentals=0
        ),
    )(x, w)


def tiles(w_ref, first_row, first_column, held_ref, sems):
    count, rows, width = held_ref.shape
    moving = [
        pltpu.make_async_copy(
            w_ref.at[pl.ds(first_row, rows), pl.ds(first_column + i * width, width)],
            held_ref.at[i],
            sems.at[i],
        )
        for i in range(count)
    ]
    for c in moving[:AHEAD]:
        c.start()
    return moving


def arrive(moving, i):
    moving[i].wait()
    if i + AHEAD < len(moving):
        moving[i + AHEAD].start()


def activate(own_ref, other_ref, scale_ref, hidden_ref):
    for lo in range(0, hidden_ref.shape[1], TILE):
        at = slice(lo, lo + TILE)
        v = (own_ref[:, at] + other_ref[:, at]) * scale_ref[:, at]
        inner = math.sqrt(2 / math.pi) * (v + 0.044715 * (v * v * v))
        hidden_ref[:, at] = (0.5 * v * (1 + jnp.tanh(inner))).astype(hidden_ref.dtype)


def down_first_kernel(own_ref, other_ref, scale_ref, w_ref, out_ref, hidden_ref, held_ref, sems):
    moving = tiles(w_ref, 0, 0, held_ref, sems)
    activate(own_ref, other_ref, scale_ref, hidden_ref)
    width = held_ref.shape[2]
    for i in range(len(moving)):
        arrive(moving, i)
        out_ref[:, i * width : (i + 1) * width] = dot(hidden_ref[...], held_ref[i])


def held(rows, width, tile):
    count = width // tile
    return [pltpu.VMEM((count, rows, tile), jnp.bfloat16), pltpu.SemaphoreType.DMA((count,))]


def cost(rows, count, width):
    return pl.CostEstimate(
        flops=2 * rows * count * width, bytes_accessed=2 * count * width, transcendentals=rows * count
    )


def down_first(own, other, scale, w):
    rows, count = own.shape
    width = w.shape[1]
    return pl.pallas_call(
        down_first_kernel,
        in_specs=[VMEM] * 3 + [HBM],
        out_specs=VMEM,
        out_shape=jax.ShapeDtypeStruct((rows, width), jnp.float32),
        scratch_shapes=[pltpu.VMEM((rows, count), jnp.bfloat16)] + held(count, width, TILE),
        compiler_params=params(13),
        cost_estimate=cost(rows, count, width),
    )(own, other, scale, w)


def over_z_kernel(
    own_ref, other_ref, scale_ref, w_ref, sum_ref,
    kept_ref, one_ref, two_ref, three_ref, hidden_ref, held_ref, sems,
):
    first_column = w_ref.shape[1] - kept_ref.shape[2]
    moving = tiles(w_ref, w_ref.shape[0] - own_ref.shape[1], first_column, held_ref, sems)
    activate(own_ref, other_ref, scale_ref, hidden_ref)
    rows = kept_ref.shape[1]
    step = held_ref.shape[2]
    for i in range(len(moving)):
        at = slice(first_column + i * step, first_column + (i + 1) * step)
        out = slice(i * step, (i + 1) * step)
        arrive(moving, i)
        terms = sum_ref[:, at] + dot(hidden_ref[...], held_ref[i])
        for j in range(2):
            base = j * 4 * rows
            kept_ref[j, :, out] = terms[base : base + rows]
            for k, ref in enumerate((one_ref, two_ref, three_ref)):
                low = base + (k + 1) * rows
                ref[j, :, out] = terms[low : low + rows].astype(jnp.bfloat16)


def over_z_terms(own, other, scale, w, total, width):
    rows, count = own.shape
    blocks = (2, rows // 8, width)
    moved = jax.ShapeDtypeStruct(blocks, jnp.bfloat16)
    return pl.pallas_call(
        over_z_kernel,
        in_specs=[VMEM] * 3 + [HBM, VMEM],
        out_specs=[VMEM] * 5,
        out_shape=[
            jax.ShapeDtypeStruct(blocks, jnp.float32),
            moved,
            moved,
            moved,
            jax.ShapeDtypeStruct((rows, count), jnp.bfloat16),
        ],
        scratch_shapes=held(count, width, width // 2),
        compiler_params=params(6),
        cost_estimate=cost(rows, count, width),
    )(own, other, scale, w, total)


def over_y_kernel(hidden_ref, w_ref, sum_ref, *out):
    kept, crossing, held_ref, sems = out[:4], out[4:8], out[8], out[9]
    moving = tiles(w_ref, w_ref.shape[0] - hidden_ref.shape[1], 0, held_ref, sems)
    rows = kept[0].shape[0]
    step = held_ref.shape[2]
    for i in range(len(moving)):
        at = slice(i * step, (i + 1) * step)
        arrive(moving, i)
        terms = sum_ref[:, at] + dot(hidden_ref[...], held_ref[i])
        for k in range(4):
            low = (4 + k) * rows
            kept[k][:, at] = terms[k * rows : (k + 1) * rows]
            crossing[k][:, at] = terms[low : low + rows].astype(jnp.bfloat16)


def over_y_terms(hidden, w, total, width):
    rows, count = hidden.shape
    block = (rows // 8, width)
    return pl.pallas_call(
        over_y_kernel,
        in_specs=[VMEM, HBM, VMEM],
        out_specs=[VMEM] * 8,
        out_shape=[jax.ShapeDtypeStruct(block, jnp.float32)] * 4
        + [jax.ShapeDtypeStruct(block, jnp.bfloat16)] * 4,
        scratch_shapes=held(count, width, width // 2),
        compiler_params=params(10),
        cost_estimate=cost(rows, count, width),
    )(hidden, w, total)


def swap_cores(x):
    return lax.ppermute(x, "fout", [(0, 1), (1, 0)])


def by_permutes(tokens, w_up, w_down, up_scale, down_scale, step_group, req_lengths):
    place = lax.axis_index("fin")
    z, y = place // 2, place % 2
    own_rows, depth = tokens.shape
    half = jnp.bfloat16

    k, j = jnp.arange(4, dtype=jnp.int32), jnp.arange(2, dtype=jnp.int32)
    block = ((z + k) % 4)[None, :] * 2 + (y ^ j)[:, None]
    rows = block.reshape(-1, 1) * own_rows + jnp.arange(own_rows, dtype=jnp.int32)[None, :]
    scale_one = scales(rows.reshape(-1), req_lengths, step_group, up_scale)
    scale_two = scales(rows[0], req_lengths, step_group, down_scale)

    w_up = pltpu.with_memory_space_constraint(w_up, pltpu.HBM)
    w_down = pltpu.with_memory_space_constraint(w_down, pltpu.HBM)
    across = move_y(tokens)
    singles = [fetch_z(tokens, k) for k in (1, 2, 3)]
    up_held = load(w_up, singles)
    single_pairs = [move_y(x) for x in singles]
    full = jnp.concatenate([tokens, *singles, across, *single_pairs])

    count = w_up.shape[1] // 2
    pre = [up(full, up_held, i * count, count) for i in range(2)]
    other = [swap_cores(p) for p in pre]
    width = w_down.shape[1] * 3 // 4 // 128 * 128
    total = down_first(pre[0], other[0], scale_one[:, :count], w_down)
    a_kept, *a_sent, hidden = over_z_terms(
        pre[1], other[1], scale_one[:, count:], w_down, total, w_down.shape[1] - width
    )
    b_terms = over_y_terms(hidden, w_down, total, width)
    b_kept, b_last, b_sent = b_terms[:4], b_terms[4], b_terms[5:]

    a_moved = [send_z(x, k + 1) for k, x in enumerate(a_sent)]
    b_across = [move_y(x) for x in b_sent]
    b_moved = [send_z((b_kept[k] + wide(b_across[k - 1])).astype(half), k) for k in (1, 2, 3)]
    a_sum = a_kept + wide(a_moved[0]) + wide(a_moved[1]) + wide(a_moved[2])
    last = move_y(jnp.concatenate([b_last, a_sum[1].astype(half)], axis=1))
    b_sum = b_kept[0] + wide(b_moved[0]) + wide(b_moved[1]) + wide(b_moved[2])
    summed = jnp.concatenate([b_sum, a_sum[0]], axis=1) + wide(last)
    return (summed * scale_two).astype(half)


def solution(mesh):
    on_device = by_permutes if mesh.shape["fin"] == 8 else by_collectives
    return jax.shard_map(
        on_device,
        mesh=mesh,
        in_specs=(
            P(("grp", "fin"), "fout"),
            P("fout", "fin"),
            P("fin", "fout"),
            P(None, "fin"),
            P(None, "fout"),
            P("grp"),
            P("grp"),
        ),
        out_specs=P(("grp", "fin"), "fout"),
        check_vma=False,
    )
```

```python
import math
import jax
import jax.numpy as jnp
from jax import lax
from jax.experimental import pallas as pl
from jax.experimental.pallas import tpu as pltpu
from jax.sharding import PartitionSpec as P


def group_table(rows, req_lengths, step_group, groups):
    place = jnp.arange(req_lengths.shape[0], dtype=jnp.int32)
    before = place[None, :] < place[:, None]
    starts = jnp.sum(jnp.where(before, req_lengths[None, :], 0), axis=1)
    ends = starts + req_lengths
    held = (rows[:, None] >= starts[None, :]) & (rows[:, None] < ends[None, :])
    row_group = jnp.sum(jnp.where(held, step_group[None, :], 0), axis=1)
    return (row_group[:, None] == jnp.arange(groups, dtype=jnp.int32)[None, :]).astype(jnp.float32)


def scales(rows, req_lengths, step_group, table):
    onehot = group_table(rows, req_lengths, step_group, table.shape[0]).astype(jnp.bfloat16)
    high = lax.reduce_precision(table, 8, 7)
    middle = lax.reduce_precision(table - high, 8, 7)
    low = table - high - middle
    return jnp.dot(
        jnp.concatenate([onehot] * 3, axis=1),
        jnp.concatenate([high, middle, low], axis=0).astype(jnp.bfloat16),
        preferred_element_type=jnp.float32,
    )


def by_collectives(tokens, w_up, w_down, up_scale, down_scale, step_group, req_lengths):
    pre = jnp.dot(
        lax.all_gather(tokens, "fin", axis=0, tiled=True), w_up, preferred_element_type=jnp.float32
    )
    total_rows = pre.shape[0]
    half_sum = lax.psum_scatter(pre, "fout", scatter_dimension=0, tiled=True)
    half_rows = half_sum.shape[0]
    rows = lax.axis_index("fout") * half_rows + jnp.arange(half_rows, dtype=jnp.int32)
    scale_one = scales(rows, req_lengths, step_group, up_scale)
    half_hidden = jax.nn.gelu(half_sum * scale_one, approximate=True).astype(jnp.bfloat16)
    hidden = lax.all_gather(half_hidden, "fout", axis=0, tiled=True)
    summed_rows = lax.psum_scatter(
        jnp.dot(hidden, w_down, preferred_element_type=jnp.float32),
        "fin",
        scatter_dimension=0,
        tiled=True,
    )
    own_rows = total_rows // lax.axis_size("fin")
    rows = lax.axis_index("fin") * own_rows + jnp.arange(own_rows, dtype=jnp.int32)
    scale_two = scales(rows, req_lengths, step_group, down_scale)
    return (summed_rows * scale_two).astype(jnp.bfloat16)


def move_y(x):
    return lax.ppermute(
        x, "fin", [(z * 2 + y, z * 2 + 1 - y) for z in range(4) for y in range(2)]
    )


def move_z(x, k):
    return lax.ppermute(
        x, "fin", [(z * 2 + y, (z ^ k) * 2 + y) for z in range(4) for y in range(2)]
    )


def wide(x):
    return x.astype(jnp.float32)


VMEM = pl.BlockSpec(memory_space=pltpu.VMEM)
HBM = pl.BlockSpec(memory_space=pltpu.HBM)
ANY = pl.BlockSpec(memory_space=pl.ANY)
TILE = 512


def params(mib):
    return pltpu.CompilerParams(vmem_limit_bytes=mib * 2**20)


def dot(a, b):
    return jnp.dot(a, b, preferred_element_type=jnp.float32)


def load_kernel(*refs):
    w_ref, out_ref, sems = refs[0], refs[-2], refs[-1]
    step = out_ref.shape[0] // sems.shape[0]
    moving = [
        pltpu.make_async_copy(
            w_ref.at[pl.ds(i * step, step)], out_ref.at[pl.ds(i * step, step)], sems.at[i]
        )
        for i in range(sems.shape[0])
    ]
    for c in moving:
        c.start()
    for c in moving:
        c.wait()


def load(w, after):
    return pl.pallas_call(
        load_kernel,
        in_specs=[HBM] + [ANY] * len(after),
        out_specs=VMEM,
        out_shape=pltpu.VMEM(w.shape, w.dtype),
        scratch_shapes=[pltpu.SemaphoreType.DMA((4,))],
        compiler_params=params(2),
        cost_estimate=pl.CostEstimate(flops=0, bytes_accessed=4 * w.size, transcendentals=0),
    )(w, *after)


def up_kernel(start, x_ref, w_ref, out_ref):
    for lo in range(0, out_ref.shape[1], TILE):
        at = slice(start + lo, start + lo + TILE)
        out_ref[:, lo : lo + TILE] = dot(x_ref[...], w_ref[:, at])


def up(x, w, start, count):
    rows = x.shape[0]
    return pl.pallas_call(
        lambda *refs: up_kernel(start, *refs),
        in_specs=[VMEM] * 2,
        out_specs=VMEM,
        out_shape=jax.ShapeDtypeStruct((rows, count), jnp.float32),
        compiler_params=params(2),
        cost_estimate=pl.CostEstimate(
            flops=2 * rows * w.shape[0] * count, bytes_accessed=4 * rows * count, transcendentals=0
        ),
    )(x, w)


def up_and_load_kernel(start, x_ref, w_ref, next_ref, out_ref, held_ref, sem):
    rows, width = held_ref.shape
    moving = pltpu.make_async_copy(
        next_ref.at[pl.ds(0, rows), pl.ds(0, width)], held_ref, sem
    )
    moving.start()
    up_kernel(start, x_ref, w_ref, out_ref)
    moving.wait()


def up_and_load(x, w, start, count, w_next, held):
    rows = x.shape[0]
    return pl.pallas_call(
        lambda *refs: up_and_load_kernel(start, *refs),
        in_specs=[VMEM, VMEM, HBM],
        out_specs=[VMEM] * 2,
        out_shape=[
            jax.ShapeDtypeStruct((rows, count), jnp.float32),
            pltpu.VMEM(held, w_next.dtype),
        ],
        scratch_shapes=[pltpu.SemaphoreType.DMA],
        compiler_params=params(2),
        cost_estimate=pl.CostEstimate(
            flops=2 * rows * w.shape[0] * count, bytes_accessed=4 * rows * count, transcendentals=0
        ),
    )(x, w, w_next)


def activate(own_ref, other_ref, scale_ref, hidden_ref):
    for lo in range(0, hidden_ref.shape[1], TILE):
        at = slice(lo, lo + TILE)
        v = (own_ref[:, at] + other_ref[:, at]) * scale_ref[:, at]
        inner = math.sqrt(2 / math.pi) * (v + 0.044715 * (v * v * v))
        hidden_ref[:, at] = (0.5 * v * (1 + jnp.tanh(inner))).astype(hidden_ref.dtype)


def down_first_kernel(
    own_ref, other_ref, scale_ref, held_ref, w_ref, out_ref, next_ref, hidden_ref, rest_ref, sems
):
    rows, width = held_ref.shape
    rest = pltpu.make_async_copy(
        w_ref.at[pl.ds(0, rows), pl.ds(width, rest_ref.shape[1])], rest_ref, sems.at[0]
    )
    step = next_ref.shape[0] // 2
    following = [
        pltpu.make_async_copy(
            w_ref.at[pl.ds(rows + i * step, step)], next_ref.at[pl.ds(i * step, step)], sems.at[1 + i]
        )
        for i in range(2)
    ]
    rest.start()
    for c in following:
        c.start()
    activate(own_ref, other_ref, scale_ref, hidden_ref)
    for lo in range(0, width, TILE):
        at = slice(lo, lo + TILE)
        out_ref[:, at] = dot(hidden_ref[...], held_ref[:, at])
    rest.wait()
    for lo in range(0, rest_ref.shape[1], TILE):
        out_ref[:, width + lo : width + lo + TILE] = dot(
            hidden_ref[...], rest_ref[:, lo : lo + TILE]
        )
    for c in following:
        c.wait()


def cost(rows, count, width):
    return pl.CostEstimate(
        flops=2 * rows * count * width, bytes_accessed=2 * count * width, transcendentals=rows * count
    )


def down_first(own, other, scale, held, w):
    rows, count = own.shape
    width = w.shape[1]
    return pl.pallas_call(
        down_first_kernel,
        in_specs=[VMEM] * 4 + [HBM],
        out_specs=[VMEM] * 2,
        out_shape=[
            jax.ShapeDtypeStruct((rows, width), jnp.float32),
            pltpu.VMEM((w.shape[0] - count, width), w.dtype),
        ],
        scratch_shapes=[
            pltpu.VMEM((rows, count), jnp.bfloat16),
            pltpu.VMEM((count, width - held.shape[1]), jnp.bfloat16),
            pltpu.SemaphoreType.DMA((3,)),
        ],
        compiler_params=params(8),
        cost_estimate=cost(rows, count, width),
    )(own, other, scale, held, w)


def over_z_kernel(
    own_ref, other_ref, scale_ref, w_ref, sum_ref,
    kept_ref, one_ref, two_ref, three_ref, hidden_ref,
):
    first_column = w_ref.shape[1] - kept_ref.shape[2]
    activate(own_ref, other_ref, scale_ref, hidden_ref)
    rows = kept_ref.shape[1]
    step = 256
    for lo in range(0, kept_ref.shape[2], step):
        at = slice(first_column + lo, first_column + lo + step)
        out = slice(lo, lo + step)
        terms = sum_ref[:, at] + dot(hidden_ref[...], w_ref[:, at])
        for j in range(2):
            base = j * 4 * rows
            kept_ref[j, :, out] = terms[base : base + rows]
            for k, ref in enumerate((one_ref, two_ref, three_ref)):
                low = base + (k + 1) * rows
                ref[j, :, out] = terms[low : low + rows].astype(jnp.bfloat16)


def over_z_terms(own, other, scale, w, total, width):
    rows, count = own.shape
    blocks = (2, rows // 8, width)
    moved = jax.ShapeDtypeStruct(blocks, jnp.bfloat16)
    return pl.pallas_call(
        over_z_kernel,
        in_specs=[VMEM] * 5,
        out_specs=[VMEM] * 5,
        out_shape=[
            jax.ShapeDtypeStruct(blocks, jnp.float32),
            moved,
            moved,
            moved,
            jax.ShapeDtypeStruct((rows, count), jnp.bfloat16),
        ],
        compiler_params=params(2),
        cost_estimate=cost(rows, count, width),
    )(own, other, scale, w, total)


def over_y_kernel(hidden_ref, w_ref, sum_ref, *out):
    kept, crossing = out[:4], out[4:]
    rows, width = kept[0].shape
    step = 256
    for lo in range(0, width, step):
        at = slice(lo, lo + step)
        terms = sum_ref[:, at] + dot(hidden_ref[...], w_ref[:, at])
        for k in range(4):
            low = (4 + k) * rows
            kept[k][:, at] = terms[k * rows : (k + 1) * rows]
            crossing[k][:, at] = terms[low : low + rows].astype(jnp.bfloat16)


def over_y_terms(hidden, w, total, width):
    rows, count = hidden.shape
    block = (rows // 8, width)
    return pl.pallas_call(
        over_y_kernel,
        in_specs=[VMEM] * 3,
        out_specs=[VMEM] * 8,
        out_shape=[jax.ShapeDtypeStruct(block, jnp.float32)] * 4
        + [jax.ShapeDtypeStruct(block, jnp.bfloat16)] * 4,
        compiler_params=params(2),
        cost_estimate=cost(rows, count, width),
    )(hidden, w, total)


def swap_cores(x):
    return lax.ppermute(x, "fout", [(0, 1), (1, 0)])


def by_permutes(tokens, w_up, w_down, up_scale, down_scale, step_group, req_lengths):
    place = lax.axis_index("fin")
    z, y = place // 2, place % 2
    own_rows, depth = tokens.shape
    half = jnp.bfloat16

    k, j = jnp.arange(4, dtype=jnp.int32), jnp.arange(2, dtype=jnp.int32)
    block = (z ^ k)[None, :] * 2 + (y ^ j)[:, None]
    rows = block.reshape(-1, 1) * own_rows + jnp.arange(own_rows, dtype=jnp.int32)[None, :]
    scale_one = scales(rows.reshape(-1), req_lengths, step_group, up_scale)
    scale_two = scales(rows[0], req_lengths, step_group, down_scale)

    w_up = pltpu.with_memory_space_constraint(w_up, pltpu.HBM)
    w_down = pltpu.with_memory_space_constraint(w_down, pltpu.HBM)
    two, one, across = move_z(tokens, 2), move_z(tokens, 1), move_y(tokens)
    up_held = load(w_up, [one, two])
    one_across, two_across, three = move_y(one), move_y(two), move_z(two, 1)
    full = jnp.concatenate(
        [tokens, one, two, three, across, one_across, two_across, move_y(three)]
    )

    count = w_up.shape[1] // 2
    first = up(full, up_held, 0, count)
    second, down_held = up_and_load(full, up_held, count, count, w_down, (count, count))
    pre = [first, second]
    other = [swap_cores(p) for p in pre]
    width = w_down.shape[1] * 3 // 4 // 128 * 128
    total, down_rest = down_first(pre[0], other[0], scale_one[:, :count], down_held, w_down)
    a_kept, *a_sent, hidden = over_z_terms(
        pre[1], other[1], scale_one[:, count:], down_rest, total, w_down.shape[1] - width
    )
    b_terms = over_y_terms(hidden, down_rest, total, width)
    b_kept, b_last, b_sent = b_terms[:4], b_terms[4], b_terms[5:]

    a_moved = [move_z(a_sent[k - 1], k) for k in (3, 2, 1)]
    b_across = [move_y(b_sent[k - 1]) for k in (3, 2, 1)]
    b_moved = [move_z((b_kept[k] + wide(b_across[3 - k])).astype(half), k) for k in (3, 2, 1)]
    a_sum = a_kept + wide(a_moved[0]) + wide(a_moved[1]) + wide(a_moved[2])
    last = move_y(jnp.concatenate([b_last, a_sum[1].astype(half)], axis=1))
    b_sum = b_kept[0] + wide(b_moved[0]) + wide(b_moved[1]) + wide(b_moved[2])
    summed = jnp.concatenate([b_sum, a_sum[0]], axis=1) + wide(last)
    return (summed * scale_two).astype(half)


def solution(mesh):
    on_device = by_permutes if mesh.shape["fin"] == 8 else by_collectives
    return jax.shard_map(
        on_device,
        mesh=mesh,
        in_specs=(
            P(("grp", "fin"), "fout"),
            P("fout", "fin"),
            P("fin", "fout"),
            P(None, "fin"),
            P(None, "fout"),
            P("grp"),
            P("grp"),
        ),
        out_specs=P(("grp", "fin"), "fout"),
        check_vma=False,
    )
```

```python
import math
import jax
import jax.numpy as jnp
from jax import lax
from jax.experimental import pallas as pl
from jax.experimental.pallas import tpu as pltpu
from jax.sharding import PartitionSpec as P


def group_table(rows, req_lengths, step_group, groups):
    place = jnp.arange(req_lengths.shape[0], dtype=jnp.int32)
    before = place[None, :] < place[:, None]
    starts = jnp.sum(jnp.where(before, req_lengths[None, :], 0), axis=1)
    ends = starts + req_lengths
    held = (rows[:, None] >= starts[None, :]) & (rows[:, None] < ends[None, :])
    row_group = jnp.sum(jnp.where(held, step_group[None, :], 0), axis=1)
    return (row_group[:, None] == jnp.arange(groups, dtype=jnp.int32)[None, :]).astype(jnp.float32)


def scales(rows, req_lengths, step_group, table):
    onehot = group_table(rows, req_lengths, step_group, table.shape[0]).astype(jnp.bfloat16)
    high = lax.reduce_precision(table, 8, 7)
    middle = lax.reduce_precision(table - high, 8, 7)
    low = table - high - middle
    return jnp.dot(
        jnp.concatenate([onehot] * 3, axis=1),
        jnp.concatenate([high, middle, low], axis=0).astype(jnp.bfloat16),
        preferred_element_type=jnp.float32,
    )


def by_collectives(tokens, w_up, w_down, up_scale, down_scale, step_group, req_lengths):
    pre = jnp.dot(
        lax.all_gather(tokens, "fin", axis=0, tiled=True), w_up, preferred_element_type=jnp.float32
    )
    total_rows = pre.shape[0]
    half_sum = lax.psum_scatter(pre, "fout", scatter_dimension=0, tiled=True)
    half_rows = half_sum.shape[0]
    rows = lax.axis_index("fout") * half_rows + jnp.arange(half_rows, dtype=jnp.int32)
    scale_one = scales(rows, req_lengths, step_group, up_scale)
    half_hidden = jax.nn.gelu(half_sum * scale_one, approximate=True).astype(jnp.bfloat16)
    hidden = lax.all_gather(half_hidden, "fout", axis=0, tiled=True)
    summed_rows = lax.psum_scatter(
        jnp.dot(hidden, w_down, preferred_element_type=jnp.float32),
        "fin",
        scatter_dimension=0,
        tiled=True,
    )
    own_rows = total_rows // lax.axis_size("fin")
    rows = lax.axis_index("fin") * own_rows + jnp.arange(own_rows, dtype=jnp.int32)
    scale_two = scales(rows, req_lengths, step_group, down_scale)
    return (summed_rows * scale_two).astype(jnp.bfloat16)


def move_y(x):
    return lax.ppermute(
        x, "fin", [(z * 2 + y, z * 2 + 1 - y) for z in range(4) for y in range(2)]
    )


def move_z(x, k):
    return lax.ppermute(
        x, "fin", [(z * 2 + y, (z ^ k) * 2 + y) for z in range(4) for y in range(2)]
    )


def wide(x):
    return x.astype(jnp.float32)


VMEM = pl.BlockSpec(memory_space=pltpu.VMEM)
HBM = pl.BlockSpec(memory_space=pltpu.HBM)
ANY = pl.BlockSpec(memory_space=pl.ANY)
TILE = 512


def params(mib):
    return pltpu.CompilerParams(vmem_limit_bytes=mib * 2**20)


def dot(a, b):
    return jnp.dot(a, b, preferred_element_type=jnp.float32)


def load_kernel(*refs):
    w_ref, out_ref, sems = refs[0], refs[-2], refs[-1]
    step = out_ref.shape[0] // sems.shape[0]
    moving = [
        pltpu.make_async_copy(
            w_ref.at[pl.ds(i * step, step)], out_ref.at[pl.ds(i * step, step)], sems.at[i]
        )
        for i in range(sems.shape[0])
    ]
    for c in moving:
        c.start()
    for c in moving:
        c.wait()


def load(w, after):
    return pl.pallas_call(
        load_kernel,
        in_specs=[HBM] + [ANY] * len(after),
        out_specs=VMEM,
        out_shape=pltpu.VMEM(w.shape, w.dtype),
        scratch_shapes=[pltpu.SemaphoreType.DMA((4,))],
        compiler_params=params(2),
        cost_estimate=pl.CostEstimate(flops=0, bytes_accessed=4 * w.size, transcendentals=0),
    )(w, *after)


def up_kernel(start, x_ref, w_ref, out_ref, sent_ref):
    for lo in range(0, out_ref.shape[1], TILE):
        at = slice(start + lo, start + lo + TILE)
        out = slice(lo, lo + TILE)
        terms = dot(x_ref[...], w_ref[:, at])
        out_ref[:, out] = terms
        sent_ref[:, out] = terms.astype(jnp.bfloat16)


def up_and_load_kernel(start, x_ref, w_ref, next_ref, out_ref, sent_ref, held_ref, sem):
    rows, width = held_ref.shape
    moving = pltpu.make_async_copy(
        next_ref.at[pl.ds(0, rows), pl.ds(start, width)], held_ref, sem
    )
    moving.start()
    up_kernel(start, x_ref, w_ref, out_ref, sent_ref)
    moving.wait()


def up(x, w, start, count, w_next, held):
    rows = x.shape[0]
    return pl.pallas_call(
        lambda *refs: up_and_load_kernel(start, *refs),
        in_specs=[VMEM, VMEM, HBM],
        out_specs=[VMEM] * 3,
        out_shape=[
            jax.ShapeDtypeStruct((rows, count), jnp.float32),
            jax.ShapeDtypeStruct((rows, count), jnp.bfloat16),
            pltpu.VMEM(held, w_next.dtype),
        ],
        scratch_shapes=[pltpu.SemaphoreType.DMA],
        compiler_params=params(2),
        cost_estimate=pl.CostEstimate(
            flops=2 * rows * w.shape[0] * count, bytes_accessed=4 * rows * count, transcendentals=0
        ),
    )(x, w, w_next)


def activate(own_ref, other_ref, scale_ref, hidden_ref):
    for lo in range(0, hidden_ref.shape[1], TILE):
        at = slice(lo, lo + TILE)
        v = (own_ref[:, at] + other_ref[:, at].astype(jnp.float32)) * scale_ref[:, at]
        inner = math.sqrt(2 / math.pi) * (v + 0.044715 * (v * v * v))
        hidden_ref[:, at] = (0.5 * v * (1 + jnp.tanh(inner))).astype(hidden_ref.dtype)


def down_first_kernel(
    own_ref, other_ref, scale_ref, left_ref, right_ref, w_ref, out_ref, next_ref, hidden_ref, sems
):
    rows, width = left_ref.shape
    step = next_ref.shape[0] // 4
    moving = [
        pltpu.make_async_copy(
            w_ref.at[pl.ds(rows + i * step, step)], next_ref.at[pl.ds(i * step, step)], sems.at[i]
        )
        for i in range(4)
    ]
    for c in moving:
        c.start()
    activate(own_ref, other_ref, scale_ref, hidden_ref)
    for i, ref in enumerate((left_ref, right_ref)):
        for lo in range(0, width, TILE):
            out_ref[:, i * width + lo : i * width + lo + TILE] = dot(
                hidden_ref[...], ref[:, lo : lo + TILE]
            )
    for c in moving:
        c.wait()


def cost(rows, count, width):
    return pl.CostEstimate(
        flops=2 * rows * count * width, bytes_accessed=2 * count * width, transcendentals=rows * count
    )


def down_first(own, other, scale, left, right, w):
    rows, count = own.shape
    width = w.shape[1]
    return pl.pallas_call(
        down_first_kernel,
        in_specs=[VMEM] * 5 + [HBM],
        out_specs=[VMEM] * 2,
        out_shape=[
            jax.ShapeDtypeStruct((rows, width), jnp.float32),
            pltpu.VMEM((w.shape[0] - count, width), w.dtype),
        ],
        scratch_shapes=[
            pltpu.VMEM((rows, count), jnp.bfloat16),
            pltpu.SemaphoreType.DMA((4,)),
        ],
        compiler_params=params(2),
        cost_estimate=cost(rows, count, width),
    )(own, other, scale, left, right, w)


def over_z_kernel(
    own_ref, other_ref, scale_ref, w_ref, sum_ref,
    kept_ref, one_ref, two_ref, three_ref, hidden_ref,
):
    first_column = w_ref.shape[1] - kept_ref.shape[2]
    activate(own_ref, other_ref, scale_ref, hidden_ref)
    rows = kept_ref.shape[1]
    step = 256
    for lo in range(0, kept_ref.shape[2], step):
        at = slice(first_column + lo, first_column + lo + step)
        out = slice(lo, lo + step)
        terms = sum_ref[:, at] + dot(hidden_ref[...], w_ref[:, at])
        for j in range(2):
            base = j * 4 * rows
            kept_ref[j, :, out] = terms[base : base + rows]
            for k, ref in enumerate((one_ref, two_ref, three_ref)):
                low = base + (k + 1) * rows
                ref[j, :, out] = terms[low : low + rows].astype(jnp.bfloat16)


def over_z_terms(own, other, scale, w, total, width):
    rows, count = own.shape
    blocks = (2, rows // 8, width)
    moved = jax.ShapeDtypeStruct(blocks, jnp.bfloat16)
    return pl.pallas_call(
        over_z_kernel,
        in_specs=[VMEM] * 5,
        out_specs=[VMEM] * 5,
        out_shape=[
            jax.ShapeDtypeStruct(blocks, jnp.float32),
            moved,
            moved,
            moved,
            jax.ShapeDtypeStruct((rows, count), jnp.bfloat16),
        ],
        compiler_params=params(2),
        cost_estimate=cost(rows, count, width),
    )(own, other, scale, w, total)


def over_y_kernel(hidden_ref, w_ref, sum_ref, *out):
    kept, crossing = out[:4], out[4:]
    rows, width = kept[0].shape
    step = 256
    for lo in range(0, width, step):
        at = slice(lo, lo + step)
        terms = sum_ref[:, at] + dot(hidden_ref[...], w_ref[:, at])
        for k in range(4):
            low = (4 + k) * rows
            kept[k][:, at] = terms[k * rows : (k + 1) * rows]
            crossing[k][:, at] = terms[low : low + rows].astype(jnp.bfloat16)


def over_y_terms(hidden, w, total, width):
    rows, count = hidden.shape
    block = (rows // 8, width)
    return pl.pallas_call(
        over_y_kernel,
        in_specs=[VMEM] * 3,
        out_specs=[VMEM] * 8,
        out_shape=[jax.ShapeDtypeStruct(block, jnp.float32)] * 4
        + [jax.ShapeDtypeStruct(block, jnp.bfloat16)] * 4,
        compiler_params=params(2),
        cost_estimate=cost(rows, count, width),
    )(hidden, w, total)


def swap_cores(x):
    return lax.ppermute(x, "fout", [(0, 1), (1, 0)])


def by_permutes(tokens, w_up, w_down, up_scale, down_scale, step_group, req_lengths):
    place = lax.axis_index("fin")
    z, y = place // 2, place % 2
    own_rows, depth = tokens.shape
    half = jnp.bfloat16

    k, j = jnp.arange(4, dtype=jnp.int32), jnp.arange(2, dtype=jnp.int32)
    block = (z ^ k)[None, :] * 2 + (y ^ j)[:, None]
    rows = block.reshape(-1, 1) * own_rows + jnp.arange(own_rows, dtype=jnp.int32)[None, :]
    scale_one = scales(rows.reshape(-1), req_lengths, step_group, up_scale)
    scale_two = scales(rows[0], req_lengths, step_group, down_scale)

    w_up = pltpu.with_memory_space_constraint(w_up, pltpu.HBM)
    w_down = pltpu.with_memory_space_constraint(w_down, pltpu.HBM)
    two, one, across = move_z(tokens, 2), move_z(tokens, 1), move_y(tokens)
    up_held = load(w_up, [one, two])
    one_across, two_across, three = move_y(one), move_y(two), move_z(two, 1)
    full = jnp.concatenate(
        [tokens, one, two, three, across, one_across, two_across, move_y(three)]
    )

    count = w_up.shape[1] // 2
    pre, sent, down_held = zip(
        *[up(full, up_held, i * count, count, w_down, (count, count)) for i in range(2)]
    )
    other = [swap_cores(x) for x in sent]
    width = w_down.shape[1] * 3 // 4 // 128 * 128
    total, down_rest = down_first(pre[0], other[0], scale_one[:, :count], *down_held, w_down)
    a_kept, *a_sent, hidden = over_z_terms(
        pre[1], other[1], scale_one[:, count:], down_rest, total, w_down.shape[1] - width
    )
    b_terms = over_y_terms(hidden, down_rest, total, width)
    b_kept, b_last, b_sent = b_terms[:4], b_terms[4], b_terms[5:]

    a_moved = [move_z(a_sent[k - 1], k) for k in (3, 2, 1)]
    b_across = [move_y(b_sent[k - 1]) for k in (3, 2, 1)]
    b_moved = [move_z((b_kept[k] + wide(b_across[3 - k])).astype(half), k) for k in (3, 2, 1)]
    a_sum = a_kept + wide(a_moved[0]) + wide(a_moved[1]) + wide(a_moved[2])
    last = move_y(jnp.concatenate([b_last, a_sum[1].astype(half)], axis=1))
    b_sum = b_kept[0] + wide(b_moved[0]) + wide(b_moved[1]) + wide(b_moved[2])
    summed = jnp.concatenate([b_sum, a_sum[0]], axis=1) + wide(last)
    return (summed * scale_two).astype(half)


def solution(mesh):
    on_device = by_permutes if mesh.shape["fin"] == 8 else by_collectives
    return jax.shard_map(
        on_device,
        mesh=mesh,
        in_specs=(
            P(("grp", "fin"), "fout"),
            P("fout", "fin"),
            P("fin", "fout"),
            P(None, "fin"),
            P(None, "fout"),
            P("grp"),
            P("grp"),
        ),
        out_specs=P(("grp", "fin"), "fout"),
        check_vma=False,
    )
```

```python
import math
import jax
import jax.numpy as jnp
from jax import lax
from jax.experimental import pallas as pl
from jax.experimental.pallas import tpu as pltpu
from jax.sharding import PartitionSpec as P


def group_table(rows, req_lengths, step_group, groups):
    place = jnp.arange(req_lengths.shape[0], dtype=jnp.int32)
    before = place[None, :] < place[:, None]
    starts = jnp.sum(jnp.where(before, req_lengths[None, :], 0), axis=1)
    ends = starts + req_lengths
    held = (rows[:, None] >= starts[None, :]) & (rows[:, None] < ends[None, :])
    row_group = jnp.sum(jnp.where(held, step_group[None, :], 0), axis=1)
    return (row_group[:, None] == jnp.arange(groups, dtype=jnp.int32)[None, :]).astype(jnp.float32)


def scales(rows, req_lengths, step_group, table):
    onehot = group_table(rows, req_lengths, step_group, table.shape[0]).astype(jnp.bfloat16)
    high = lax.reduce_precision(table, 8, 7)
    middle = lax.reduce_precision(table - high, 8, 7)
    low = table - high - middle
    return jnp.dot(
        jnp.concatenate([onehot] * 3, axis=1),
        jnp.concatenate([high, middle, low], axis=0).astype(jnp.bfloat16),
        preferred_element_type=jnp.float32,
    )


def by_collectives(tokens, w_up, w_down, up_scale, down_scale, step_group, req_lengths):
    pre = jnp.dot(
        lax.all_gather(tokens, "fin", axis=0, tiled=True), w_up, preferred_element_type=jnp.float32
    )
    total_rows = pre.shape[0]
    half_sum = lax.psum_scatter(pre, "fout", scatter_dimension=0, tiled=True)
    half_rows = half_sum.shape[0]
    rows = lax.axis_index("fout") * half_rows + jnp.arange(half_rows, dtype=jnp.int32)
    scale_one = scales(rows, req_lengths, step_group, up_scale)
    half_hidden = jax.nn.gelu(half_sum * scale_one, approximate=True).astype(jnp.bfloat16)
    hidden = lax.all_gather(half_hidden, "fout", axis=0, tiled=True)
    summed_rows = lax.psum_scatter(
        jnp.dot(hidden, w_down, preferred_element_type=jnp.float32),
        "fin",
        scatter_dimension=0,
        tiled=True,
    )
    own_rows = total_rows // lax.axis_size("fin")
    rows = lax.axis_index("fin") * own_rows + jnp.arange(own_rows, dtype=jnp.int32)
    scale_two = scales(rows, req_lengths, step_group, down_scale)
    return (summed_rows * scale_two).astype(jnp.bfloat16)


def move_y(x):
    return lax.ppermute(
        x, "fin", [(z * 2 + y, z * 2 + 1 - y) for z in range(4) for y in range(2)]
    )


def move_z(x, k):
    return lax.ppermute(
        x, "fin", [(z * 2 + y, (z ^ k) * 2 + y) for z in range(4) for y in range(2)]
    )


def wide(x):
    return x.astype(jnp.float32)


VMEM = pl.BlockSpec(memory_space=pltpu.VMEM)
HBM = pl.BlockSpec(memory_space=pltpu.HBM)
ANY = pl.BlockSpec(memory_space=pl.ANY)
TILE = 512


def params(mib):
    return pltpu.CompilerParams(vmem_limit_bytes=mib * 2**20)


def dot(a, b):
    return jnp.dot(a, b, preferred_element_type=jnp.float32)


def load_kernel(*refs):
    w_ref, out_ref, sems = refs[0], refs[-2], refs[-1]
    step = out_ref.shape[0] // sems.shape[0]
    moving = [
        pltpu.make_async_copy(
            w_ref.at[pl.ds(i * step, step)], out_ref.at[pl.ds(i * step, step)], sems.at[i]
        )
        for i in range(sems.shape[0])
    ]
    for c in moving:
        c.start()
    for c in moving:
        c.wait()


def load(w, after):
    return pl.pallas_call(
        load_kernel,
        in_specs=[HBM] + [ANY] * len(after),
        out_specs=VMEM,
        out_shape=pltpu.VMEM(w.shape, w.dtype),
        scratch_shapes=[pltpu.SemaphoreType.DMA((4,))],
        compiler_params=params(2),
        cost_estimate=pl.CostEstimate(flops=0, bytes_accessed=4 * w.size, transcendentals=0),
    )(w, *after)


def up_kernel(start, x_ref, w_ref, out_ref, sent_ref):
    for lo in range(0, out_ref.shape[1], TILE):
        at = slice(start + lo, start + lo + TILE)
        out = slice(lo, lo + TILE)
        terms = dot(x_ref[...], w_ref[:, at])
        out_ref[:, out] = terms
        sent_ref[:, out] = terms.astype(jnp.bfloat16)


def up_and_load_kernel(start, x_ref, w_ref, next_ref, out_ref, sent_ref, held_ref, sem):
    rows, width = held_ref.shape
    moving = pltpu.make_async_copy(
        next_ref.at[pl.ds(0, rows), pl.ds(start, width)], held_ref, sem
    )
    moving.start()
    up_kernel(start, x_ref, w_ref, out_ref, sent_ref)
    moving.wait()


def up(x, w, start, count, w_next, held):
    rows = x.shape[0]
    return pl.pallas_call(
        lambda *refs: up_and_load_kernel(start, *refs),
        in_specs=[VMEM, VMEM, HBM],
        out_specs=[VMEM] * 3,
        out_shape=[
            jax.ShapeDtypeStruct((rows, count), jnp.float32),
            jax.ShapeDtypeStruct((rows, count), jnp.bfloat16),
            pltpu.VMEM(held, w_next.dtype),
        ],
        scratch_shapes=[pltpu.SemaphoreType.DMA],
        compiler_params=params(2),
        cost_estimate=pl.CostEstimate(
            flops=2 * rows * w.shape[0] * count, bytes_accessed=4 * rows * count, transcendentals=0
        ),
    )(x, w, w_next)


def activate(own_ref, other_ref, scale_ref, hidden_ref):
    for lo in range(0, hidden_ref.shape[1], TILE):
        at = slice(lo, lo + TILE)
        v = (own_ref[:, at] + other_ref[:, at].astype(jnp.float32)) * scale_ref[:, at]
        inner = math.sqrt(2 / math.pi) * (v + 0.044715 * (v * v * v))
        hidden_ref[:, at] = (0.5 * v * (1 + jnp.tanh(inner))).astype(hidden_ref.dtype)


def down_first_kernel(
    own_ref, other_ref, scale_ref, left_ref, right_ref, w_ref, out_ref, next_ref, hidden_ref, sems
):
    rows, width = left_ref.shape
    step = next_ref.shape[0] // 4
    moving = [
        pltpu.make_async_copy(
            w_ref.at[pl.ds(rows + i * step, step)], next_ref.at[pl.ds(i * step, step)], sems.at[i]
        )
        for i in range(4)
    ]
    for c in moving:
        c.start()
    activate(own_ref, other_ref, scale_ref, hidden_ref)
    for i, ref in enumerate((left_ref, right_ref)):
        for lo in range(0, width, TILE):
            out_ref[:, i * width + lo : i * width + lo + TILE] = dot(
                hidden_ref[...], ref[:, lo : lo + TILE]
            )
    for c in moving:
        c.wait()


def cost(rows, count, width):
    return pl.CostEstimate(
        flops=2 * rows * count * width, bytes_accessed=2 * count * width, transcendentals=rows * count
    )


def down_first(own, other, scale, left, right, w):
    rows, count = own.shape
    width = w.shape[1]
    return pl.pallas_call(
        down_first_kernel,
        in_specs=[VMEM] * 5 + [HBM],
        out_specs=[VMEM] * 2,
        out_shape=[
            jax.ShapeDtypeStruct((rows, width), jnp.float32),
            pltpu.VMEM((w.shape[0] - count, width), w.dtype),
        ],
        scratch_shapes=[
            pltpu.VMEM((rows, count), jnp.bfloat16),
            pltpu.SemaphoreType.DMA((4,)),
        ],
        compiler_params=params(2),
        cost_estimate=cost(rows, count, width),
    )(own, other, scale, left, right, w)


def over_z_kernel(
    own_ref, other_ref, scale_ref, w_ref, sum_ref,
    kept_ref, one_ref, two_ref, three_ref, hidden_ref,
):
    first_column = w_ref.shape[1] - kept_ref.shape[2]
    activate(own_ref, other_ref, scale_ref, hidden_ref)
    rows = kept_ref.shape[1]
    step = 256
    for lo in range(0, kept_ref.shape[2], step):
        at = slice(first_column + lo, first_column + lo + step)
        out = slice(lo, lo + step)
        terms = sum_ref[:, at] + dot(hidden_ref[...], w_ref[:, at])
        for j in range(2):
            base = j * 4 * rows
            kept_ref[j, :, out] = terms[base : base + rows]
            for k, ref in enumerate((one_ref, two_ref, three_ref)):
                low = base + (k + 1) * rows
                ref[j, :, out] = terms[low : low + rows].astype(jnp.bfloat16)


def over_z_terms(own, other, scale, w, total, width):
    rows, count = own.shape
    blocks = (2, rows // 8, width)
    moved = jax.ShapeDtypeStruct(blocks, jnp.bfloat16)
    return pl.pallas_call(
        over_z_kernel,
        in_specs=[VMEM] * 5,
        out_specs=[VMEM] * 5,
        out_shape=[
            jax.ShapeDtypeStruct(blocks, jnp.float32),
            moved,
            moved,
            moved,
            jax.ShapeDtypeStruct((rows, count), jnp.bfloat16),
        ],
        compiler_params=params(2),
        cost_estimate=cost(rows, count, width),
    )(own, other, scale, w, total)


def over_y_kernel(hidden_ref, w_ref, sum_ref, *out):
    kept, crossing = out[:4], out[4:]
    rows, width = kept[0].shape
    step = 256
    for lo in range(0, width, step):
        at = slice(lo, lo + step)
        terms = sum_ref[:, at] + dot(hidden_ref[...], w_ref[:, at])
        for k in range(4):
            low = (4 + k) * rows
            kept[k][:, at] = terms[k * rows : (k + 1) * rows]
            crossing[k][:, at] = terms[low : low + rows].astype(jnp.bfloat16)


def over_y_terms(hidden, w, total, width):
    rows, count = hidden.shape
    block = (rows // 8, width)
    return pl.pallas_call(
        over_y_kernel,
        in_specs=[VMEM] * 3,
        out_specs=[VMEM] * 8,
        out_shape=[jax.ShapeDtypeStruct(block, jnp.float32)] * 4
        + [jax.ShapeDtypeStruct(block, jnp.bfloat16)] * 4,
        compiler_params=params(2),
        cost_estimate=cost(rows, count, width),
    )(hidden, w, total)


def swap_cores(x):
    return lax.ppermute(x, "fout", [(0, 1), (1, 0)])


def by_permutes(tokens, w_up, w_down, up_scale, down_scale, step_group, req_lengths):
    place = lax.axis_index("fin")
    z, y = place // 2, place % 2
    own_rows, depth = tokens.shape
    half = jnp.bfloat16

    k, j = jnp.arange(4, dtype=jnp.int32), jnp.arange(2, dtype=jnp.int32)
    block = (z ^ k)[None, :] * 2 + (y ^ j)[:, None]
    rows = block.reshape(-1, 1) * own_rows + jnp.arange(own_rows, dtype=jnp.int32)[None, :]
    scale_one = scales(rows.reshape(-1), req_lengths, step_group, up_scale)
    scale_two = scales(rows[0], req_lengths, step_group, down_scale)

    w_up = pltpu.with_memory_space_constraint(w_up, pltpu.HBM)
    w_down = pltpu.with_memory_space_constraint(w_down, pltpu.HBM)
    two, one, across = move_z(tokens, 2), move_z(tokens, 1), move_y(tokens)
    up_held = load(w_up, [one, two])
    two_across, one_across, three = move_y(two), move_y(one), move_z(two, 1)
    half_rows = own_rows // 2
    three_across = [move_y(three[:half_rows]), move_z(two_across[half_rows:], 1)]
    full = jnp.concatenate(
        [tokens, one, two, three, across, one_across, two_across, *three_across]
    )

    count = w_up.shape[1] // 2
    pre, sent, down_held = zip(
        *[up(full, up_held, i * count, count, w_down, (count, count)) for i in range(2)]
    )
    other = [swap_cores(x) for x in sent]
    width = w_down.shape[1] * 3 // 4 // 128 * 128
    total, down_rest = down_first(pre[0], other[0], scale_one[:, :count], *down_held, w_down)
    a_kept, *a_sent, hidden = over_z_terms(
        pre[1], other[1], scale_one[:, count:], down_rest, total, w_down.shape[1] - width
    )
    b_terms = over_y_terms(hidden, down_rest, total, width)
    b_kept, b_last, b_sent = b_terms[:4], b_terms[4], b_terms[5:]

    a_moved = [move_z(a_sent[k - 1], k) for k in (2, 3, 1)]
    b_across = [move_y(b_sent[k - 1]) for k in (2, 3, 1)]
    b_moved = [move_z((b_kept[k] + wide(b_across[(2, 3, 1).index(k)])).astype(half), k) for k in (2, 3, 1)]
    a_sum = a_kept + wide(a_moved[0]) + wide(a_moved[1]) + wide(a_moved[2])
    last = move_y(jnp.concatenate([b_last, a_sum[1].astype(half)], axis=1))
    b_sum = b_kept[0] + wide(b_moved[0]) + wide(b_moved[1]) + wide(b_moved[2])
    summed = jnp.concatenate([b_sum, a_sum[0]], axis=1) + wide(last)
    return (summed * scale_two).astype(half)


def solution(mesh):
    on_device = by_permutes if mesh.shape["fin"] == 8 else by_collectives
    return jax.shard_map(
        on_device,
        mesh=mesh,
        in_specs=(
            P(("grp", "fin"), "fout"),
            P("fout", "fin"),
            P("fin", "fout"),
            P(None, "fin"),
            P(None, "fout"),
            P("grp"),
            P("grp"),
        ),
        out_specs=P(("grp", "fin"), "fout"),
        check_vma=False,
    )
```

```python
import math
import jax
import jax.numpy as jnp
from jax import lax
from jax.experimental import pallas as pl
from jax.experimental.pallas import tpu as pltpu
from jax.sharding import PartitionSpec as P


def group_table(rows, req_lengths, step_group, groups):
    place = jnp.arange(req_lengths.shape[0], dtype=jnp.int32)
    before = place[None, :] < place[:, None]
    starts = jnp.sum(jnp.where(before, req_lengths[None, :], 0), axis=1)
    ends = starts + req_lengths
    held = (rows[:, None] >= starts[None, :]) & (rows[:, None] < ends[None, :])
    row_group = jnp.sum(jnp.where(held, step_group[None, :], 0), axis=1)
    return (row_group[:, None] == jnp.arange(groups, dtype=jnp.int32)[None, :]).astype(jnp.float32)


def scales(rows, req_lengths, step_group, table):
    onehot = group_table(rows, req_lengths, step_group, table.shape[0]).astype(jnp.bfloat16)
    high = lax.reduce_precision(table, 8, 7)
    middle = lax.reduce_precision(table - high, 8, 7)
    low = table - high - middle
    return jnp.dot(
        jnp.concatenate([onehot] * 3, axis=1),
        jnp.concatenate([high, middle, low], axis=0).astype(jnp.bfloat16),
        preferred_element_type=jnp.float32,
    )


def by_collectives(tokens, w_up, w_down, up_scale, down_scale, step_group, req_lengths):
    pre = jnp.dot(
        lax.all_gather(tokens, "fin", axis=0, tiled=True), w_up, preferred_element_type=jnp.float32
    )
    total_rows = pre.shape[0]
    half_sum = lax.psum_scatter(pre, "fout", scatter_dimension=0, tiled=True)
    half_rows = half_sum.shape[0]
    rows = lax.axis_index("fout") * half_rows + jnp.arange(half_rows, dtype=jnp.int32)
    scale_one = scales(rows, req_lengths, step_group, up_scale)
    half_hidden = jax.nn.gelu(half_sum * scale_one, approximate=True).astype(jnp.bfloat16)
    hidden = lax.all_gather(half_hidden, "fout", axis=0, tiled=True)
    summed_rows = lax.psum_scatter(
        jnp.dot(hidden, w_down, preferred_element_type=jnp.float32),
        "fin",
        scatter_dimension=0,
        tiled=True,
    )
    own_rows = total_rows // lax.axis_size("fin")
    rows = lax.axis_index("fin") * own_rows + jnp.arange(own_rows, dtype=jnp.int32)
    scale_two = scales(rows, req_lengths, step_group, down_scale)
    return (summed_rows * scale_two).astype(jnp.bfloat16)


def move_y(x):
    return lax.ppermute(
        x, "fin", [(z * 2 + y, z * 2 + 1 - y) for z in range(4) for y in range(2)]
    )


def move_z(x, k):
    return lax.ppermute(
        x, "fin", [(z * 2 + y, (z ^ k) * 2 + y) for z in range(4) for y in range(2)]
    )


def wide(x):
    return x.astype(jnp.float32)


VMEM = pl.BlockSpec(memory_space=pltpu.VMEM)
HBM = pl.BlockSpec(memory_space=pltpu.HBM)
ANY = pl.BlockSpec(memory_space=pl.ANY)
TILE = 512


def params(mib):
    return pltpu.CompilerParams(vmem_limit_bytes=mib * 2**20)


def dot(a, b):
    return jnp.dot(a, b, preferred_element_type=jnp.float32)


def load_kernel(*refs):
    w_ref, out_ref, sems = refs[0], refs[-2], refs[-1]
    step = out_ref.shape[0] // sems.shape[0]
    moving = [
        pltpu.make_async_copy(
            w_ref.at[pl.ds(i * step, step)], out_ref.at[pl.ds(i * step, step)], sems.at[i]
        )
        for i in range(sems.shape[0])
    ]
    for c in moving:
        c.start()
    for c in moving:
        c.wait()


def load(w, after):
    return pl.pallas_call(
        load_kernel,
        in_specs=[HBM] + [ANY] * len(after),
        out_specs=VMEM,
        out_shape=pltpu.VMEM(w.shape, w.dtype),
        scratch_shapes=[pltpu.SemaphoreType.DMA((4,))],
        compiler_params=params(2),
        cost_estimate=pl.CostEstimate(flops=0, bytes_accessed=4 * w.size, transcendentals=0),
    )(w, *after)


def up_kernel(start, x_ref, w_ref, out_ref, sent_ref):
    for lo in range(0, out_ref.shape[1], TILE):
        at = slice(start + lo, start + lo + TILE)
        out = slice(lo, lo + TILE)
        terms = dot(x_ref[...], w_ref[:, at])
        out_ref[:, out] = terms
        sent_ref[:, out] = terms.astype(jnp.bfloat16)


def up_and_load_kernel(start, x_ref, w_ref, next_ref, out_ref, sent_ref, held_ref, sem):
    rows, width = held_ref.shape
    moving = pltpu.make_async_copy(
        next_ref.at[pl.ds(0, rows), pl.ds(start, width)], held_ref, sem
    )
    moving.start()
    up_kernel(start, x_ref, w_ref, out_ref, sent_ref)
    moving.wait()


def up(x, w, start, count, w_next, held):
    rows = x.shape[0]
    return pl.pallas_call(
        lambda *refs: up_and_load_kernel(start, *refs),
        in_specs=[VMEM, VMEM, HBM],
        out_specs=[VMEM] * 3,
        out_shape=[
            jax.ShapeDtypeStruct((rows, count), jnp.float32),
            jax.ShapeDtypeStruct((rows, count), jnp.bfloat16),
            pltpu.VMEM(held, w_next.dtype),
        ],
        scratch_shapes=[pltpu.SemaphoreType.DMA],
        compiler_params=params(2),
        cost_estimate=pl.CostEstimate(
            flops=2 * rows * w.shape[0] * count, bytes_accessed=4 * rows * count, transcendentals=0
        ),
    )(x, w, w_next)


def activate(own_ref, other_ref, scale_ref, hidden_ref):
    for lo in range(0, hidden_ref.shape[1], TILE):
        at = slice(lo, lo + TILE)
        v = (own_ref[:, at] + other_ref[:, at].astype(jnp.float32)) * scale_ref[:, at]
        inner = math.sqrt(2 / math.pi) * (v + 0.044715 * (v * v * v))
        hidden_ref[:, at] = (0.5 * v * (1 + jnp.tanh(inner))).astype(hidden_ref.dtype)


def down_first_kernel(
    own_ref, other_ref, scale_ref, left_ref, right_ref, w_ref, out_ref, next_ref, hidden_ref, sems
):
    rows, width = left_ref.shape
    step = next_ref.shape[0] // 4
    moving = [
        pltpu.make_async_copy(
            w_ref.at[pl.ds(rows + i * step, step)], next_ref.at[pl.ds(i * step, step)], sems.at[i]
        )
        for i in range(4)
    ]
    for c in moving:
        c.start()
    activate(own_ref, other_ref, scale_ref, hidden_ref)
    for i, ref in enumerate((left_ref, right_ref)):
        for lo in range(0, width, TILE):
            out_ref[:, i * width + lo : i * width + lo + TILE] = dot(
                hidden_ref[...], ref[:, lo : lo + TILE]
            )
    for c in moving:
        c.wait()


def cost(rows, count, width):
    return pl.CostEstimate(
        flops=2 * rows * count * width, bytes_accessed=2 * count * width, transcendentals=rows * count
    )


def down_first(own, other, scale, left, right, w):
    rows, count = own.shape
    width = w.shape[1]
    return pl.pallas_call(
        down_first_kernel,
        in_specs=[VMEM] * 5 + [HBM],
        out_specs=[VMEM] * 2,
        out_shape=[
            jax.ShapeDtypeStruct((rows, width), jnp.float32),
            pltpu.VMEM((w.shape[0] - count, width), w.dtype),
        ],
        scratch_shapes=[
            pltpu.VMEM((rows, count), jnp.bfloat16),
            pltpu.SemaphoreType.DMA((4,)),
        ],
        compiler_params=params(2),
        cost_estimate=cost(rows, count, width),
    )(own, other, scale, left, right, w)


def over_z_kernel(
    own_ref, other_ref, scale_ref, w_ref, sum_ref,
    kept_ref, one_ref, two_ref, three_ref, hidden_ref,
):
    first_column = w_ref.shape[1] - kept_ref.shape[2]
    activate(own_ref, other_ref, scale_ref, hidden_ref)
    rows = kept_ref.shape[1]
    step = 256
    for lo in range(0, kept_ref.shape[2], step):
        at = slice(first_column + lo, first_column + lo + step)
        out = slice(lo, lo + step)
        terms = sum_ref[:, at] + dot(hidden_ref[...], w_ref[:, at])
        for j in range(2):
            base = j * 4 * rows
            kept_ref[j, :, out] = terms[base : base + rows]
            for k, ref in enumerate((one_ref, two_ref, three_ref)):
                low = base + (k + 1) * rows
                ref[j, :, out] = terms[low : low + rows].astype(jnp.bfloat16)


def over_z_terms(own, other, scale, w, total, width):
    rows, count = own.shape
    blocks = (2, rows // 8, width)
    moved = jax.ShapeDtypeStruct(blocks, jnp.bfloat16)
    return pl.pallas_call(
        over_z_kernel,
        in_specs=[VMEM] * 5,
        out_specs=[VMEM] * 5,
        out_shape=[
            jax.ShapeDtypeStruct(blocks, jnp.float32),
            moved,
            moved,
            moved,
            jax.ShapeDtypeStruct((rows, count), jnp.bfloat16),
        ],
        compiler_params=params(2),
        cost_estimate=cost(rows, count, width),
    )(own, other, scale, w, total)


def over_y_kernel(hidden_ref, w_ref, sum_ref, *out):
    kept, crossing = out[:4], out[4:]
    rows, width = kept[0].shape
    step = 256
    for lo in range(0, width, step):
        at = slice(lo, lo + step)
        terms = sum_ref[:, at] + dot(hidden_ref[...], w_ref[:, at])
        for k in range(4):
            low = (4 + k) * rows
            kept[k][:, at] = terms[k * rows : (k + 1) * rows]
            crossing[k][:, at] = terms[low : low + rows].astype(jnp.bfloat16)


def over_y_terms(hidden, w, total, width):
    rows, count = hidden.shape
    block = (rows // 8, width)
    return pl.pallas_call(
        over_y_kernel,
        in_specs=[VMEM] * 3,
        out_specs=[VMEM] * 8,
        out_shape=[jax.ShapeDtypeStruct(block, jnp.float32)] * 4
        + [jax.ShapeDtypeStruct(block, jnp.bfloat16)] * 4,
        compiler_params=params(2),
        cost_estimate=cost(rows, count, width),
    )(hidden, w, total)


def swap_cores(x):
    return lax.ppermute(x, "fout", [(0, 1), (1, 0)])


def by_permutes(tokens, w_up, w_down, up_scale, down_scale, step_group, req_lengths):
    place = lax.axis_index("fin")
    z, y = place // 2, place % 2
    own_rows, depth = tokens.shape
    half = jnp.bfloat16

    k, j = jnp.arange(4, dtype=jnp.int32), jnp.arange(2, dtype=jnp.int32)
    block = (z ^ k)[None, :] * 2 + (y ^ j)[:, None]
    rows = block.reshape(-1, 1) * own_rows + jnp.arange(own_rows, dtype=jnp.int32)[None, :]
    scale_one = scales(rows.reshape(-1), req_lengths, step_group, up_scale)
    scale_two = scales(rows[0], req_lengths, step_group, down_scale)

    w_up = pltpu.with_memory_space_constraint(w_up, pltpu.HBM)
    w_down = pltpu.with_memory_space_constraint(w_down, pltpu.HBM)
    two, one, across = move_z(tokens, 2), move_z(tokens, 1), move_y(tokens)
    up_held = load(w_up, [one, two])
    two_across, one_across, three = move_y(two), move_y(one), move_z(two, 1)
    half_rows = own_rows // 2
    three_across = [move_y(three[:half_rows]), move_z(two_across[half_rows:], 1)]
    full = jnp.concatenate(
        [tokens, one, two, three, across, one_across, two_across, *three_across]
    )

    count = w_up.shape[1] // 2
    pre, sent, down_held = zip(
        *[up(full, up_held, i * count, count, w_down, (count, count)) for i in range(2)]
    )
    other = [swap_cores(x) for x in sent]
    width = w_down.shape[1] * 3 // 4 // 128 * 128
    total, down_rest = down_first(pre[0], other[0], scale_one[:, :count], *down_held, w_down)
    a_kept, *a_sent, hidden = over_z_terms(
        pre[1], other[1], scale_one[:, count:], down_rest, total, w_down.shape[1] - width
    )
    b_terms = over_y_terms(hidden, down_rest, total, width)
    b_kept, b_last, b_sent = b_terms[:4], b_terms[4], b_terms[5:]

    a_moved = [move_z(a_sent[k - 1], k) for k in (2, 3, 1)]
    b_across = [move_y(b_sent[k - 1]) for k in (3, 2, 1)]
    b_moved = [move_z((b_kept[k] + wide(b_across[(3, 2, 1).index(k)])).astype(half), k) for k in (3, 2, 1)]
    a_sum = a_kept + wide(a_moved[0]) + wide(a_moved[1]) + wide(a_moved[2])
    last = move_y(jnp.concatenate([b_last, a_sum[1].astype(half)], axis=1))
    b_sum = b_kept[0] + wide(b_moved[0]) + wide(b_moved[1]) + wide(b_moved[2])
    summed = jnp.concatenate([b_sum, a_sum[0]], axis=1) + wide(last)
    return (summed * scale_two).astype(half)


def solution(mesh):
    on_device = by_permutes if mesh.shape["fin"] == 8 else by_collectives
    return jax.shard_map(
        on_device,
        mesh=mesh,
        in_specs=(
            P(("grp", "fin"), "fout"),
            P("fout", "fin"),
            P("fin", "fout"),
            P(None, "fin"),
            P(None, "fout"),
            P("grp"),
            P("grp"),
        ),
        out_specs=P(("grp", "fin"), "fout"),
        check_vma=False,
    )
```
